32 devices in a mesh: case: 2 (over y), panel: 4 (over z), slab: 2 (over x), obs: 2 (over core).
Axes of the slice: x: 2, y: 2, z: 4, core: 2. Of those that a mesh axis runs over, the one named last changes fastest.
Arguments:
- loading: bfloat16 [65536, 512], P(('case', 'panel'), 'slab'), parts along dimension 0, may hold values from -6 to 6
- green: bfloat16 [128, 32768], P(('case', 'obs'), 'panel'), parts along dimension 0, may hold values from -0.03125 to 0.03125
- delays: int32 [128, 2048], P(('case', 'obs'), 'panel'), parts along dimension 0, may hold values from 0 to 120
- offsets: int32 [128, 2048], P(('case', 'obs'), 'panel'), parts along dimension 0, may hold values from 0 to 7
- live_groups: int32 [8], P('case'), parts along dimension 0, may hold values from 1 to 4, as said below
Outputs:
- signal: float32 [128, 512], P(('case', 'obs'), 'slab'), parts along dimension 0
The draws below stay inside these ranges and needn't reach their ends.
There are 2 independent parts, one for each index of `case`. The reference program is written for one: setup_inputs(seed, part) draws one part's arguments, and reference() takes and returns one part's arrays. A program takes and returns all parts, laid end to end along the dimension named above; each array names one. Nothing has to cross between parts.
Inputs may be any that keep to these rules, and one draw needn't show every extreme that they name: `live_groups`: in every draw some sector has all 4 groups live while the sector 4/2 positions away has one.
All inputs are finite; a program needn't handle non-finite values.
Results may differ from the reference program's by a relative error of at most 0.0034.
Values may be sent and summed in bfloat16 or wider, within the bound.
No kernel may reach another device: no remote copies, remote signals or barrier semaphores. Data moves between devices by JAX's collectives and lax.ppermute only.
A program may use at most 64 MiB of HBM per device.

```python
import jax
import jax.numpy as jnp
from jax import lax

OBS = 64
BP = 16
GB = 128
GROUPS = 4
LAGS = 128
SECTORS = 4
PANELS = 32768
BLOCKS = 2048
TSAMP = 512


def draw_live_groups(key, part):
    first_key, second_key, third_key = jax.random.split(jax.random.fold_in(key, 17), 3)
    heavy = jax.random.randint(first_key, (SECTORS,), 0, 3) == 0
    extra = jax.random.randint(second_key, (SECTORS,), 2, GROUPS + 1)
    counts = jnp.where(heavy, extra, 1).astype(jnp.int32)
    picked = jax.random.randint(third_key, (), 0, SECTORS)
    counts = counts.at[picked].set(GROUPS)
    partner = jnp.bitwise_xor(picked, SECTORS // 2)
    counts = counts.at[partner].set(1)
    return counts.astype(jnp.int32)


def touch_ends(entries, stream_key, least, high):
    longest = entries.shape.index(max(entries.shape))
    spots = []
    for shift in (0, 1):
        where = [jax.random.randint(jax.random.fold_in(stream_key, axis), (), 0, length) for axis, length in enumerate(entries.shape)]
        where[longest] = (where[longest] + shift) % entries.shape[longest]
        spots.append(tuple(where))
    return entries.at[spots[0]].set(least).at[spots[1]].set(high)


def level_of(stream_key, shape, shards, smallest, largest):
    factor_of, own = 1.0, jax.random.fold_in(stream_key, 6)
    for axis_at, blocks in shards:
        steps = jnp.exp(jax.random.uniform(jax.random.fold_in(own, axis_at), (blocks,), jnp.float32, smallest / len(shards), largest / len(shards)))
        factor_of = factor_of * jnp.repeat(steps, shape[axis_at] // blocks).reshape([-1 if axis == axis_at else 1 for axis in range(len(shape))])
    return factor_of


def normal_values(key, shape, spread, reach, pieces=(), kind=jnp.bfloat16):
    level = level_of(key, shape, pieces, -0.22, 0.18) if pieces else 1.0
    values = jax.random.normal(key, shape, jnp.float32) * spread * level
    return jnp.minimum(jnp.maximum(values, -reach), reach).astype(kind)


def setup_inputs(seed: int = 0, part: int = 0) -> dict:
    arg_keys = jax.random.split(jax.random.key(seed), 6)
    own_keys = jax.random.split(jax.random.fold_in(arg_keys[5], part), 6)
    loading = normal_values(own_keys[0], (PANELS, TSAMP), 1.0, 6.0, ((0, 4), (1, 2)))
    green = normal_values(own_keys[1], (OBS, PANELS), PANELS ** -0.5, 0.03125, ((0, 2), (1, 4)))
    delays = touch_ends(jax.random.randint(own_keys[2], (OBS, BLOCKS), 0, LAGS - 7), jax.random.fold_in(own_keys[2], 1), 0, (LAGS - 7) - 1).astype(jnp.int32)
    offsets = touch_ends(jax.random.randint(own_keys[3], (OBS, BLOCKS), 0, 8), jax.random.fold_in(own_keys[3], 1), 0, 7).astype(jnp.int32)
    live_groups = draw_live_groups(jax.random.fold_in(jax.random.fold_in(arg_keys[5], part), 71), part)
    return dict(loading=loading, green=green, delays=delays, offsets=offsets, live_groups=live_groups)


def lagrange_weights(offset_part):
    position = 3.0 + offset_part.astype(jnp.float32) / 8.0
    weights = []
    for tap in range(8):
        factor = jnp.ones_like(position)
        for other in range(8):
            if other != tap:
                factor = factor * (position - other) / (tap - other)
        weights.append(factor)
    return weights


def build_table(delay_part, offset_part, lag_count):
    lag_index = jnp.arange(lag_count, dtype=jnp.int32)[None, :, None]
    relative = lag_index - delay_part.astype(jnp.int32)[:, None, :]
    weights = lagrange_weights(offset_part)
    table_sum = jnp.zeros(relative.shape, jnp.float32)
    for tap in range(8):
        table_sum = table_sum + jnp.where(relative == tap, weights[tap][:, None, :], 0.0)
    return table_sum.astype(jnp.bfloat16)


def reference(loading, green, delays, offsets, live_groups):
    samples = loading.shape[1]
    group_count = SECTORS * GROUPS
    grouped_load = loading.reshape(group_count, GB, BP, samples)
    grouped_green = jnp.moveaxis(green.reshape(OBS, group_count, GB, BP), 1, 0)
    grouped_delay = jnp.moveaxis(delays.reshape(OBS, group_count, GB), 1, 0)
    grouped_offset = jnp.moveaxis(offsets.reshape(OBS, group_count, GB), 1, 0)
    fft_length = samples + LAGS

    def compute(group_index):
        block_signal = jnp.einsum("obp,bpt->bot", grouped_green[group_index].astype(jnp.float32),
                                  grouped_load[group_index].astype(jnp.float32)).astype(jnp.bfloat16)
        block_signal = lax.optimization_barrier(block_signal).astype(jnp.float32)
        lag_table = build_table(grouped_delay[group_index], grouped_offset[group_index], LAGS)
        lag_table = lax.optimization_barrier(lag_table).astype(jnp.float32)
        signal_spectrum = jnp.fft.rfft(block_signal, fft_length, axis=2)
        table_spectrum = jnp.fft.rfft(jnp.transpose(lag_table, (2, 0, 1)), fft_length, axis=2)
        combined = jnp.sum(signal_spectrum * table_spectrum, axis=0)
        return jnp.fft.irfft(combined, fft_length, axis=1)[:, :samples].astype(jnp.float32)

    def skipped(group_index):
        return jnp.zeros((OBS, samples), jnp.float32)

    def step_group(carried, group_index):
        sector = group_index // GROUPS
        is_live = live_groups[sector] > group_index % GROUPS
        return carried + lax.cond(is_live, compute, skipped, group_index), None

    start_sum = jnp.zeros((OBS, samples), jnp.float32)
    signal, unused = lax.scan(step_group, start_sum, jnp.arange(group_count, dtype=jnp.int32))
    return signal
```

```python
import functools

import jax
import jax.numpy as jnp
from jax import lax
from jax.experimental import pallas as pl
from jax.experimental.pallas import tpu as pltpu
from jax.sharding import PartitionSpec as P

BP = 16
GB = 128
LAGS = 128
TAPS = 8
ROWS = 16
LANES = 128
CHUNK = 256


def passed_along(block, axis, distance):
    devices = range(lax.axis_size(axis))
    route = [(i - distance, i) for i in devices if i - distance in devices]
    return lax.ppermute(block, axis, route)


def weight_lanes():
    lane = lax.broadcasted_iota(jnp.int32, (8, LANES), 1)
    tap = (lane % ROWS).astype(jnp.float32)
    position = 3.0 + (lane // ROWS).astype(jnp.float32) / 8.0
    top = jnp.ones_like(position)
    bottom = jnp.ones_like(position)
    for other in range(TAPS):
        here = tap == other
        top = top * jnp.where(here, 1.0, position - other)
        bottom = bottom * jnp.where(here, 1.0, tap - other)
    return jnp.where(tap < TAPS, top / bottom, 0.0)


def shifted_add(upper, lower, distance):
    lane = lax.broadcasted_iota(jnp.int32, (8, LANES), 1)
    rows = lower[0].shape[0]
    wraps = (lane < distance)[None]
    turned = [pltpu.roll(tile, distance, 1).reshape(rows // 8, 8, LANES) for tile in lower]
    zero = jnp.zeros((rows // 8, 8, LANES), jnp.float32)
    out = []
    for at in range(max(len(upper), len(lower) + 1)):
        before = turned[at - 1] if 0 < at <= len(turned) else zero
        here = turned[at] if at < len(turned) else zero
        moved = jnp.where(wraps, before, here).reshape(rows, LANES)
        out.append(moved + upper[at] if at < len(upper) else moved)
    return out


def far_kernel(groups, live_hbm, load_hbm, green_hbm, delay_hbm, offset_hbm, main_ref, tail_ref,
               live_s, load_v, green_v, green_f, delay_v, offset_v, taps_v, place_v, sig_v, part_v,
               small_sem, load_sem):
    observers = green_v.shape[0]
    samples = load_v.shape[1]
    panels = load_v.shape[0]
    blocks = panels // BP
    pieces = load_sem.shape[0]
    piece = panels // pieces
    pairs = groups // 2
    chunk_blocks = CHUNK // BP

    small = [
        pltpu.make_async_copy(src, dst, small_sem.at[i])
        for i, (src, dst) in enumerate(
            [(live_hbm, live_s), (delay_hbm, delay_v), (offset_hbm, offset_v), (green_hbm, green_v)]
        )
    ]
    for copy in small:
        copy.start()
    loads = [
        pltpu.make_async_copy(load_hbm.at[pl.ds(i * piece, piece)], load_v.at[pl.ds(i * piece, piece)], load_sem.at[i])
        for i in range(pieces)
    ]
    for copy in loads:
        copy.start()

    weights = weight_lanes()
    for copy in small[:3]:
        copy.wait()
    count = live_s[lax.axis_index("panel")]
    live_pairs = (count + 1) // 2

    row = lax.broadcasted_iota(jnp.int32, (ROWS, LANES), 0)

    def prepare(band, carry):
        rows = pl.ds(pl.multiple_of(band * 8, 8), 8)
        for g in range(groups):
            cols = pl.ds(g * LANES, LANES)
            dead = jnp.where(g < count, 0, -1024)
            delays = delay_v[rows, cols]
            offsets = offset_v[rows, cols]
            for r in range(8):
                o = band * 8 + r
                delay = jnp.broadcast_to(delays[r:r + 1], (ROWS, LANES))
                offset = jnp.broadcast_to(offsets[r:r + 1], (ROWS, LANES))
                entry = ((row - delay) & (ROWS - 1)) + offset * ROWS
                values = [jnp.take_along_axis(weights, entry[h:h + 8], axis=1) for h in (0, 8)]
                taps_v[o, :, cols] = jnp.concatenate(values, 0).astype(jnp.bfloat16)
                place = ((delay - row + (ROWS - 1)) >> 4) + dead
                place_v[o, :, cols] = place.astype(jnp.float32).astype(jnp.bfloat16)
        return carry

    lax.fori_loop(0, observers // 8, prepare, 0)

    small[3].wait()
    for c in range(panels // CHUNK):
        green_f[c] = green_v[:, c * CHUNK:(c + 1) * CHUNK].astype(jnp.float32)
    for copy in loads:
        copy.wait()

    own = lax.broadcasted_iota(jnp.int32, (ROWS, CHUNK), 1) // BP == lax.broadcasted_iota(jnp.int32, (ROWS, CHUNK), 0)
    own = own.astype(jnp.float32).astype(jnp.bfloat16)

    def first(c, carry):
        spread = []
        for o in range(observers):
            line = jnp.broadcast_to(green_f[c, o:o + 1, :], (ROWS, CHUNK)).astype(jnp.bfloat16)
            spread.append(line * own)
        block = jnp.dot(
            jnp.concatenate(spread, 0),
            load_v[pl.ds(pl.multiple_of(c * CHUNK, CHUNK), CHUNK), :],
            preferred_element_type=jnp.float32,
        ).astype(jnp.bfloat16)
        at = pl.ds(pl.multiple_of(c * chunk_blocks, chunk_blocks), chunk_blocks)
        for o in range(observers):
            sig_v[o, at, :] = block[o * ROWS:(o + 1) * ROWS]
        return carry

    lax.fori_loop(0, live_pairs * (2 * GB // chunk_blocks), first, 0)

    def second(depth, o, carry):
        taps = taps_v[o, :, :depth]
        place = place_v[o, :, :depth]
        table = jnp.concatenate(
            [jnp.where(place == jnp.bfloat16(j), taps, jnp.bfloat16(0)) for j in range(LAGS // ROWS)], 0
        )
        lagged = jnp.dot(table, sig_v[o, :depth, :], preferred_element_type=jnp.float32)
        tiles = [lagged[:, t * LANES:(t + 1) * LANES] for t in range(samples // LANES)]
        half = LAGS // 2
        while half >= 8:
            tiles = shifted_add([t[:half] for t in tiles], [t[half:] for t in tiles], half)[: samples // LANES + 1]
            half //= 2
        for t, tile in enumerate(tiles):
            part_v[t, pl.ds(pl.multiple_of(o * 8, 8), 8), :] = tile
        return carry

    for pair in range(1, pairs + 1):
        @pl.when(live_pairs == pair)
        def _():
            lax.fori_loop(0, observers, functools.partial(second, pair * 2 * GB), 0, unroll=2)

    tiles_out = samples // LANES + 1
    total = [part_v[t, pl.ds(0, observers, stride=8), :] for t in range(tiles_out)]
    for s in range(1, 8):
        line = [part_v[t, pl.ds(s, observers, stride=8), :] for t in range(tiles_out)]
        total = shifted_add(total, line, s)[:tiles_out]
    for t in range(samples // LANES):
        main_ref[:, t * LANES:(t + 1) * LANES] = total[t]
    tail_ref[...] = total[-1]


def far_partial(loading, green, delays, offsets, live_groups):
    panels, samples = loading.shape
    observers = green.shape[0]
    blocks = panels // BP
    groups = blocks // GB
    pieces = panels // CHUNK // 2
    far = pl.BlockSpec(memory_space=pltpu.HBM)
    vmem = pl.BlockSpec(memory_space=pltpu.VMEM)
    return pl.pallas_call(
        functools.partial(far_kernel, groups),
        out_shape=(
            jax.ShapeDtypeStruct((observers, samples), jnp.float32),
            jax.ShapeDtypeStruct((observers, LAGS), jnp.float32),
        ),
        in_specs=[far] * 5,
        out_specs=(vmem, vmem),
        scratch_shapes=[
            pltpu.SMEM(live_groups.shape, jnp.int32),
            pltpu.VMEM((panels, samples), jnp.bfloat16),
            pltpu.VMEM((observers, panels), jnp.bfloat16),
            pltpu.VMEM((panels // CHUNK, observers, CHUNK), jnp.float32),
            pltpu.VMEM((observers, blocks), jnp.int32),
            pltpu.VMEM((observers, blocks), jnp.int32),
            pltpu.VMEM((observers, ROWS, blocks), jnp.bfloat16),
            pltpu.VMEM((observers, ROWS, blocks), jnp.bfloat16),
            pltpu.VMEM((observers, blocks, samples), jnp.bfloat16),
            pltpu.VMEM((samples // LANES + 1, observers * 8, LANES), jnp.float32),
            pltpu.SemaphoreType.DMA((4,)),
            pltpu.SemaphoreType.DMA((pieces,)),
        ],
        compiler_params=pltpu.CompilerParams(vmem_limit_bytes=60 * 1024 * 1024),
        name="far_partial",
    )(live_groups, loading, green, delays, offsets)


def shards(loading, green, delays, offsets, live_groups):
    main, tail = far_partial(loading, green, delays, offsets, live_groups)
    samples = main.shape[1]
    carried = passed_along(tail, "slab", 1)
    part = main + jnp.pad(carried, ((0, 0), (0, samples - LAGS)))
    sectors = lax.axis_size("panel")
    reach = 1
    while reach < sectors:
        part = part + lax.ppermute(part, "panel", [(i, i ^ reach) for i in range(sectors)])
        reach *= 2
    return part


def solution(mesh):
    placed = (
        P(("case", "panel"), "slab"),
        P(("case", "obs"), "panel"),
        P(("case", "obs"), "panel"),
        P(("case", "obs"), "panel"),
        P("case"),
    )
    return jax.shard_map(
        shards, mesh=mesh, in_specs=placed, out_specs=P(("case", "obs"), "slab"), check_vma=False
    )
```

```python
import functools

import jax
import jax.numpy as jnp
from jax import lax
from jax.experimental import pallas as pl
from jax.experimental.pallas import tpu as pltpu
from jax.sharding import PartitionSpec as P

BP = 16
GB = 128
LAGS = 128
TAPS = 8
ROWS = 16
LANES = 128
CHUNK = 256


def passed_along(block, axis, distance):
    devices = range(lax.axis_size(axis))
    route = [(i - distance, i) for i in devices if i - distance in devices]
    return lax.ppermute(block, axis, route)


def weight_lanes():
    lane = lax.broadcasted_iota(jnp.int32, (8, LANES), 1)
    tap = (lane % ROWS).astype(jnp.float32)
    position = 3.0 + (lane // ROWS).astype(jnp.float32) / 8.0
    top = jnp.ones_like(position)
    bottom = jnp.ones_like(position)
    for other in range(TAPS):
        here = tap == other
        top = top * jnp.where(here, 1.0, position - other)
        bottom = bottom * jnp.where(here, 1.0, tap - other)
    return jnp.where(tap < TAPS, top / bottom, 0.0)


def shifted_add(upper, lower, distance):
    lane = lax.broadcasted_iota(jnp.int32, (8, LANES), 1)
    rows = lower[0].shape[0]
    wraps = (lane < distance)[None]
    turned = [pltpu.roll(tile, distance, 1).reshape(rows // 8, 8, LANES) for tile in lower]
    zero = jnp.zeros((rows // 8, 8, LANES), jnp.float32)
    out = []
    for at in range(max(len(upper), len(lower) + 1)):
        before = turned[at - 1] if 0 < at <= len(turned) else zero
        here = turned[at] if at < len(turned) else zero
        moved = jnp.where(wraps, before, here).reshape(rows, LANES)
        out.append(moved + upper[at] if at < len(upper) else moved)
    return out


def far_kernel(groups, live_hbm, load_hbm, green_hbm, delay_hbm, offset_hbm, main_ref, tail_ref,
               live_s, load_v, green_v, green_f, delay_v, offset_v, taps_v, place_v, sig_v, part_v,
               small_sem, load_sem):
    observers = green_v.shape[0]
    samples = load_v.shape[1]
    panels = load_v.shape[0]
    blocks = panels // BP
    pieces = load_sem.shape[0]
    piece = panels // pieces
    pairs = groups // 2
    chunk_blocks = CHUNK // BP

    small = [
        pltpu.make_async_copy(src, dst, small_sem.at[i])
        for i, (src, dst) in enumerate(
            [(live_hbm, live_s), (delay_hbm, delay_v), (offset_hbm, offset_v), (green_hbm, green_v)]
        )
    ]
    for copy in small:
        copy.start()
    loads = [
        pltpu.make_async_copy(load_hbm.at[pl.ds(i * piece, piece)], load_v.at[pl.ds(i * piece, piece)], load_sem.at[i])
        for i in range(pieces)
    ]
    loads[0].start()

    weights = weight_lanes()
    for copy in small[:3]:
        copy.wait()
    for copy in loads[1:]:
        copy.start()
    count = live_s[lax.axis_index("panel")]
    live_pairs = (count + 1) // 2

    row = lax.broadcasted_iota(jnp.int32, (ROWS, LANES), 0)

    def prepare(band, carry):
        rows = pl.ds(pl.multiple_of(band * 8, 8), 8)
        for g in range(groups):
            cols = pl.ds(g * LANES, LANES)
            dead = jnp.where(g < count, 0, -1024)
            delays = delay_v[rows, cols]
            offsets = offset_v[rows, cols]
            for r in range(8):
                o = band * 8 + r
                delay = jnp.broadcast_to(delays[r:r + 1], (ROWS, LANES))
                offset = jnp.broadcast_to(offsets[r:r + 1], (ROWS, LANES))
                entry = ((row - delay) & (ROWS - 1)) + offset * ROWS
                values = [jnp.take_along_axis(weights, entry[h:h + 8], axis=1) for h in (0, 8)]
                taps_v[o, :, cols] = jnp.concatenate(values, 0).astype(jnp.bfloat16)
                place = ((delay - row + (ROWS - 1)) >> 4) + dead
                place_v[o, :, cols] = place.astype(jnp.float32).astype(jnp.bfloat16)
        return carry

    lax.fori_loop(0, observers // 8, prepare, 0)

    small[3].wait()
    for c in range(panels // CHUNK):
        green_f[c] = green_v[:, c * CHUNK:(c + 1) * CHUNK].astype(jnp.float32)
    own = lax.broadcasted_iota(jnp.int32, (ROWS, CHUNK), 1) // BP == lax.broadcasted_iota(jnp.int32, (ROWS, CHUNK), 0)
    own = own.astype(jnp.float32).astype(jnp.bfloat16)

    per = piece // CHUNK

    def piece_here(i):
        pltpu.make_async_copy(load_hbm.at[pl.ds(0, piece)], load_v.at[pl.ds(0, piece)], load_sem.at[i]).wait()

    def first(i, carry):
        piece_here(i)
        for c in range(per):
            chunk = i * per + c
            spread = []
            for o in range(observers):
                line = jnp.broadcast_to(green_f[chunk, o:o + 1, :], (ROWS, CHUNK)).astype(jnp.bfloat16)
                spread.append(line * own)
            block = jnp.dot(
                jnp.concatenate(spread, 0),
                load_v[pl.ds(pl.multiple_of(chunk * CHUNK, CHUNK), CHUNK), :],
                preferred_element_type=jnp.float32,
            ).astype(jnp.bfloat16)
            at = pl.ds(pl.multiple_of(chunk * chunk_blocks, chunk_blocks), chunk_blocks)
            for o in range(observers):
                sig_v[o, at, :] = block[o * ROWS:(o + 1) * ROWS]
        return carry

    def unused(i, carry):
        piece_here(i)
        return carry

    wanted = live_pairs * 2
    lax.fori_loop(0, wanted, first, 0)
    lax.fori_loop(wanted, pieces, unused, 0)

    def second(depth, o, carry):
        taps = taps_v[o, :, :depth]
        place = place_v[o, :, :depth]
        table = jnp.concatenate(
            [jnp.where(place == jnp.bfloat16(j), taps, jnp.bfloat16(0)) for j in range(LAGS // ROWS)], 0
        )
        lagged = jnp.dot(table, sig_v[o, :depth, :], preferred_element_type=jnp.float32)
        tiles = [lagged[:, t * LANES:(t + 1) * LANES] for t in range(samples // LANES)]
        half = LAGS // 2
        while half >= 8:
            tiles = shifted_add([t[:half] for t in tiles], [t[half:] for t in tiles], half)[: samples // LANES + 1]
            half //= 2
        for t, tile in enumerate(tiles):
            part_v[t, pl.ds(pl.multiple_of(o * 8, 8), 8), :] = tile
        return carry

    for pair in range(1, pairs + 1):
        @pl.when(live_pairs == pair)
        def _():
            lax.fori_loop(0, observers, functools.partial(second, pair * 2 * GB), 0, unroll=observers // 2)

    tiles_out = samples // LANES + 1
    total = [part_v[t, pl.ds(0, observers, stride=8), :] for t in range(tiles_out)]
    for s in range(1, 8):
        line = [part_v[t, pl.ds(s, observers, stride=8), :] for t in range(tiles_out)]
        total = shifted_add(total, line, s)[:tiles_out]
    for t in range(samples // LANES):
        main_ref[:, t * LANES:(t + 1) * LANES] = total[t]
    tail_ref[...] = total[-1]


def far_partial(loading, green, delays, offsets, live_groups):
    panels, samples = loading.shape
    observers = green.shape[0]
    blocks = panels // BP
    groups = blocks // GB
    pieces = groups
    operands = (live_groups, loading, green, delays, offsets)
    far = pl.BlockSpec(memory_space=pltpu.HBM)
    vmem = pl.BlockSpec(memory_space=pltpu.VMEM)
    return pl.pallas_call(
        functools.partial(far_kernel, groups),
        out_shape=(
            jax.ShapeDtypeStruct((observers, samples), jnp.float32),
            jax.ShapeDtypeStruct((observers, LAGS), jnp.float32),
        ),
        in_specs=[far] * 5,
        out_specs=(vmem, vmem),
        scratch_shapes=[
            pltpu.SMEM(live_groups.shape, jnp.int32),
            pltpu.VMEM((panels, samples), jnp.bfloat16),
            pltpu.VMEM((observers, panels), jnp.bfloat16),
            pltpu.VMEM((panels // CHUNK, observers, CHUNK), jnp.float32),
            pltpu.VMEM((observers, blocks), jnp.int32),
            pltpu.VMEM((observers, blocks), jnp.int32),
            pltpu.VMEM((observers, ROWS, blocks), jnp.bfloat16),
            pltpu.VMEM((observers, ROWS, blocks), jnp.bfloat16),
            pltpu.VMEM((observers, blocks, samples), jnp.bfloat16),
            pltpu.VMEM((samples // LANES + 1, observers * 8, LANES), jnp.float32),
            pltpu.SemaphoreType.DMA((4,)),
            pltpu.SemaphoreType.DMA((pieces,)),
        ],
        compiler_params=pltpu.CompilerParams(vmem_limit_bytes=24 * 1024 * 1024),
        name="far_partial",
    )(*[pltpu.with_memory_space_constraint(x, pltpu.HBM) for x in operands])


def shards(loading, green, delays, offsets, live_groups):
    main, tail = far_partial(loading, green, delays, offsets, live_groups)
    samples = main.shape[1]
    carried = passed_along(tail, "slab", 1)
    part = main + jnp.pad(carried, ((0, 0), (0, samples - LAGS)))
    sectors = lax.axis_size("panel")
    reach = 1
    while reach < sectors:
        part = part + lax.ppermute(part, "panel", [(i, i ^ reach) for i in range(sectors)])
        reach *= 2
    return part


def solution(mesh):
    placed = (
        P(("case", "panel"), "slab"),
        P(("case", "obs"), "panel"),
        P(("case", "obs"), "panel"),
        P(("case", "obs"), "panel"),
        P("case"),
    )
    return jax.shard_map(
        shards, mesh=mesh, in_specs=placed, out_specs=P(("case", "obs"), "slab"), check_vma=False
    )
```

```python
import functools

import jax
import jax.numpy as jnp
from jax import lax
from jax.experimental import pallas as pl
from jax.experimental.pallas import tpu as pltpu
from jax.sharding import PartitionSpec as P

BP = 16
GB = 128
LAGS = 128
TAPS = 8
ROWS = 16
LANES = 128
CHUNK = 256


def next_slab(block):
    slabs = lax.axis_size("slab")
    got = lax.ppermute(block, "slab", [(i, (i + 1) % slabs) for i in range(slabs)])
    return jnp.where(lax.axis_index("slab") > 0, got, 0.0)


def panel_sum(part):
    sectors = lax.axis_size("panel")
    reach = 1
    while reach < sectors:
        steps = [k * reach for k in (1, 2, 3) if k * reach < sectors]
        got = [lax.ppermute(part, "panel", [(i, i ^ step) for i in range(sectors)]) for step in steps]
        part = part + functools.reduce(jnp.add, got)
        reach *= len(got) + 1
    return part


def weight_lanes():
    lane = lax.broadcasted_iota(jnp.int32, (8, LANES), 1)
    tap = (lane % ROWS).astype(jnp.float32)
    position = 3.0 + (lane // ROWS).astype(jnp.float32) / 8.0
    top = jnp.ones_like(position)
    bottom = jnp.ones_like(position)
    for other in range(TAPS):
        here = tap == other
        top = top * jnp.where(here, 1.0, position - other)
        bottom = bottom * jnp.where(here, 1.0, tap - other)
    return jnp.where(tap < TAPS, top / bottom, 0.0)


def far_kernel(groups, live_hbm, load_hbm, green_hbm, delay_hbm, offset_hbm, main_ref, tail_ref,
               live_s, load_v, green_v, green_f, delay_v, offset_v, taps_v, place_v, sig_v, part_v,
               small_sem, load_sem):
    observers = green_v.shape[0]
    samples = load_v.shape[1]
    panels = load_v.shape[0]
    blocks = panels // BP
    pieces = load_sem.shape[0]
    piece = panels // pieces
    pairs = groups // 2
    chunk_blocks = CHUNK // BP

    small = [
        pltpu.make_async_copy(src, dst, small_sem.at[i])
        for i, (src, dst) in enumerate(
            [(live_hbm, live_s), (green_hbm, green_v), (delay_hbm, delay_v), (offset_hbm, offset_v)]
        )
    ]
    loads = [
        pltpu.make_async_copy(load_hbm.at[pl.ds(i * piece, piece)], load_v.at[pl.ds(i * piece, piece)], load_sem.at[i])
        for i in range(pieces)
    ]
    for copy in small:
        copy.start()
    loads[0].start()
    weights = weight_lanes()
    for copy in small:
        copy.wait()
    for copy in loads[1:]:
        copy.start()
    count = live_s[lax.axis_index("panel")]
    live_pairs = (count + 1) // 2

    row = lax.broadcasted_iota(jnp.int32, (ROWS, LANES), 0)

    def prepare(band):
        rows = pl.ds(pl.multiple_of(band * 8, 8), 8)
        for g in range(groups):
            cols = pl.ds(g * LANES, LANES)
            dead = jnp.where(g < count, 0, -1024)
            delays = delay_v[rows, cols]
            offsets = offset_v[rows, cols]
            for r in range(8):
                o = band * 8 + r
                delay = jnp.broadcast_to(delays[r:r + 1], (ROWS, LANES))
                offset = jnp.broadcast_to(offsets[r:r + 1], (ROWS, LANES))
                entry = ((row - delay) & (ROWS - 1)) + offset * ROWS
                values = [jnp.take_along_axis(weights, entry[h:h + 8], axis=1) for h in (0, 8)]
                taps_v[o, :, cols] = jnp.concatenate(values, 0).astype(jnp.bfloat16)
                place = ((delay - row + (ROWS - 1)) >> 4) + dead
                place_v[o, :, cols] = place.astype(jnp.float32).astype(jnp.bfloat16)

    for c in range(panels // CHUNK):
        green_f[c] = green_v[:, c * CHUNK:(c + 1) * CHUNK].astype(jnp.float32)
    own = lax.broadcasted_iota(jnp.int32, (ROWS, CHUNK), 1) // BP == lax.broadcasted_iota(jnp.int32, (ROWS, CHUNK), 0)
    own = own.astype(jnp.float32).astype(jnp.bfloat16)

    per = piece // CHUNK
    bands = observers // 8 // pieces

    def piece_here(i):
        pltpu.make_async_copy(load_hbm.at[pl.ds(0, piece)], load_v.at[pl.ds(0, piece)], load_sem.at[i]).wait()

    def first(i, carry):
        piece_here(i)
        for band in range(bands):
            prepare(i * bands + band)
        for c in range(per):
            chunk = i * per + c
            spread = []
            for o in range(observers):
                line = jnp.broadcast_to(green_f[chunk, o:o + 1, :], (ROWS, CHUNK)).astype(jnp.bfloat16)
                spread.append(line * own)
            block = jnp.dot(
                jnp.concatenate(spread, 0),
                load_v[pl.ds(pl.multiple_of(chunk * CHUNK, CHUNK), CHUNK), :],
                preferred_element_type=jnp.float32,
            ).astype(jnp.bfloat16)
            at = pl.ds(pl.multiple_of(chunk * chunk_blocks, chunk_blocks), chunk_blocks)
            for o in range(observers):
                sig_v[o, at, :] = block[o * ROWS:(o + 1) * ROWS]
        return carry

    def unused(i, carry):
        piece_here(i)
        for band in range(bands):
            prepare(i * bands + band)
        return carry

    wanted = live_pairs * 2
    lax.fori_loop(0, wanted, first, 0)
    lax.fori_loop(wanted, pieces, unused, 0)

    tiles_out = samples // LANES + 1
    lane = lax.broadcasted_iota(jnp.int32, (8, LANES), 1)
    lag = lax.broadcasted_iota(jnp.int32, (8, LANES), 0)
    passed = [lane < lag + j * 8 for j in range(LAGS // 8)]

    def second(depth, o, carry):
        taps = taps_v[o, :, :depth]
        place = place_v[o, :, :depth]
        table = jnp.concatenate(
            [jnp.where(place == jnp.bfloat16(j), taps, jnp.bfloat16(0)) for j in range(LAGS // ROWS)], 0
        )
        lagged = jnp.dot(table, sig_v[o, :depth, :], preferred_element_type=jnp.float32)
        parts = [jnp.zeros((8, LANES), jnp.float32)] * tiles_out
        for j in range(LAGS // 8):
            turned = [
                pltpu.roll(lagged[j * 8:(j + 1) * 8, t * LANES:(t + 1) * LANES], j * 8, 1, stride=1, stride_axis=0)
                for t in range(samples // LANES)
            ]
            before, here = [0.0] + turned, turned + [0.0]
            parts = [part + jnp.where(passed[j], before[t], here[t]) for t, part in enumerate(parts)]
        for t, tile in enumerate(parts):
            part_v[t, pl.ds(pl.multiple_of(o * 8, 8), 8), :] = tile
        return carry

    for pair in range(1, pairs + 1):
        @pl.when(live_pairs == pair)
        def _():
            lax.fori_loop(0, observers, functools.partial(second, pair * 2 * GB), 0, unroll=(observers if pair == 2 else observers // 2))

    for t in range(tiles_out):
        total = part_v[t, pl.ds(0, observers, stride=8), :]
        for r in range(1, 8):
            total = total + part_v[t, pl.ds(r, observers, stride=8), :]
        if t < tiles_out - 1:
            main_ref[:, t * LANES:(t + 1) * LANES] = total
        else:
            tail_ref[...] = total


def far_partial(loading, green, delays, offsets, live_groups):
    panels, samples = loading.shape
    observers = green.shape[0]
    blocks = panels // BP
    groups = blocks // GB
    pieces = groups
    operands = (live_groups, loading, green, delays, offsets)
    far = pl.BlockSpec(memory_space=pltpu.HBM)
    vmem = pl.BlockSpec(memory_space=pltpu.VMEM)
    return pl.pallas_call(
        functools.partial(far_kernel, groups),
        out_shape=(
            jax.ShapeDtypeStruct((observers, samples), jnp.float32),
            jax.ShapeDtypeStruct((observers, LAGS), jnp.float32),
        ),
        in_specs=[far] * 5,
        out_specs=(vmem, vmem),
        scratch_shapes=[
            pltpu.SMEM(live_groups.shape, jnp.int32),
            pltpu.VMEM((panels, samples), jnp.bfloat16),
            pltpu.VMEM((observers, panels), jnp.bfloat16),
            pltpu.VMEM((panels // CHUNK, observers, CHUNK), jnp.float32),
            pltpu.VMEM((observers, blocks), jnp.int32),
            pltpu.VMEM((observers, blocks), jnp.int32),
            pltpu.VMEM((observers, ROWS, blocks), jnp.bfloat16),
            pltpu.VMEM((observers, ROWS, blocks), jnp.bfloat16),
            pltpu.VMEM((observers, blocks, samples), jnp.bfloat16),
            pltpu.VMEM((samples // LANES + 1, observers * 8, LANES), jnp.float32),
            pltpu.SemaphoreType.DMA((4,)),
            pltpu.SemaphoreType.DMA((pieces,)),
        ],
        compiler_params=pltpu.CompilerParams(vmem_limit_bytes=24 * 1024 * 1024),
        name="far_partial",
    )(*[pltpu.with_memory_space_constraint(x, pltpu.HBM) for x in operands])


def shards(loading, green, delays, offsets, live_groups):
    main, tail = far_partial(loading, green, delays, offsets, live_groups)
    samples = main.shape[1]
    carried = next_slab(tail)
    return panel_sum(main + jnp.pad(carried, ((0, 0), (0, samples - LAGS))))


def solution(mesh):
    placed = (
        P(("case", "panel"), "slab"),
        P(("case", "obs"), "panel"),
        P(("case", "obs"), "panel"),
        P(("case", "obs"), "panel"),
        P("case"),
    )
    return jax.shard_map(
        shards, mesh=mesh, in_specs=placed, out_specs=P(("case", "obs"), "slab"), check_vma=False
    )
```

```python
import functools

import jax
import jax.numpy as jnp
from jax import lax
from jax.experimental import pallas as pl
from jax.experimental.pallas import tpu as pltpu
from jax.sharding import PartitionSpec as P

BP = 16
GB = 128
LAGS = 128
TAPS = 8
ROWS = 16
LANES = 128
CHUNK = 256


def from_sector(block, step):
    sectors = lax.axis_size("panel")
    return lax.ppermute(block, "panel", [(i, i ^ step) for i in range(sectors)])


def from_slab_before(block, step):
    sectors, slabs = lax.axis_size("panel"), lax.axis_size("slab")
    route = [
        (p * slabs + q, (p ^ step) * slabs + (q + 1) % slabs) for p in range(sectors) for q in range(slabs)
    ]
    return lax.ppermute(block, ("panel", "slab"), route)


def weight_lanes():
    lane = lax.broadcasted_iota(jnp.int32, (8, LANES), 1)
    tap = (lane % ROWS).astype(jnp.float32)
    position = 3.0 + (lane // ROWS).astype(jnp.float32) / 8.0
    top = jnp.ones_like(position)
    bottom = jnp.ones_like(position)
    for other in range(TAPS):
        here = tap == other
        top = top * jnp.where(here, 1.0, position - other)
        bottom = bottom * jnp.where(here, 1.0, tap - other)
    return jnp.where(tap < TAPS, top / bottom, 0.0)


def at_chunk(start, size):
    return pl.ds(start if isinstance(start, int) else pl.multiple_of(start, size), size)


def far_kernel(groups, live_hbm, load_hbm, green_hbm, delay_hbm, offset_hbm, main_ref, tail_ref,
               live_s, load_v, green_v, green_f, delay_v, offset_v, taps_v, place_v, sig_v, part_v,
               small_sem, load_sem):
    observers = green_v.shape[0]
    samples = load_v.shape[1]
    panels = load_v.shape[0]
    blocks = panels // BP
    pieces = load_sem.shape[0]
    piece = panels // pieces
    chunk_blocks = CHUNK // BP

    small = [
        pltpu.make_async_copy(src, dst, small_sem.at[i])
        for i, (src, dst) in enumerate(
            [(live_hbm, live_s), (green_hbm, green_v), (delay_hbm, delay_v), (offset_hbm, offset_v)]
        )
    ]
    loads = [
        pltpu.make_async_copy(load_hbm.at[pl.ds(i * piece, piece)], load_v.at[pl.ds(i * piece, piece)], load_sem.at[i])
        for i in range(pieces)
    ]
    for copy in small:
        copy.start()
    loads[0].start()
    weights = weight_lanes()
    for copy in small:
        copy.wait()
    for copy in loads[1:]:
        copy.start()
    count = live_s[lax.axis_index("panel")]

    row = lax.broadcasted_iota(jnp.int32, (ROWS, LANES), 0)

    def prepare(band, held):
        rows = at_chunk(band * 8, 8)
        for g in range(held):
            cols = pl.ds(g * LANES, LANES)
            dead = jnp.where(g < count, 0, -1024)
            delays = delay_v[rows, cols]
            offsets = offset_v[rows, cols]
            for r in range(8):
                o = band * 8 + r
                delay = jnp.broadcast_to(delays[r:r + 1], (ROWS, LANES))
                offset = jnp.broadcast_to(offsets[r:r + 1], (ROWS, LANES))
                entry = ((row - delay) & (ROWS - 1)) + offset * ROWS
                values = [jnp.take_along_axis(weights, entry[h:h + 8], axis=1) for h in (0, 8)]
                taps_v[o, :, cols] = jnp.concatenate(values, 0).astype(jnp.bfloat16)
                place = ((delay - row + (ROWS - 1)) >> 4) + dead
                place_v[o, :, cols] = place.astype(jnp.float32).astype(jnp.bfloat16)

    for c in range(panels // CHUNK):
        green_f[c] = green_v[:, c * CHUNK:(c + 1) * CHUNK].astype(jnp.float32)
    own = lax.broadcasted_iota(jnp.int32, (ROWS, CHUNK), 1) // BP == lax.broadcasted_iota(jnp.int32, (ROWS, CHUNK), 0)
    own = own.astype(jnp.float32).astype(jnp.bfloat16)

    per = piece // CHUNK
    bands = observers // 8 // pieces

    def piece_here(i):
        pltpu.make_async_copy(load_hbm.at[pl.ds(0, piece)], load_v.at[pl.ds(0, piece)], load_sem.at[i]).wait()

    def first(i):
        for c in range(per):
            chunk = i * per + c
            spread = []
            for o in range(observers):
                line = jnp.broadcast_to(green_f[chunk, o:o + 1, :], (ROWS, CHUNK)).astype(jnp.bfloat16)
                spread.append(line * own)
            block = jnp.dot(
                jnp.concatenate(spread, 0),
                load_v[at_chunk(chunk * CHUNK, CHUNK), :],
                preferred_element_type=jnp.float32,
            ).astype(jnp.bfloat16)
            at = at_chunk(chunk * chunk_blocks, chunk_blocks)
            for o in range(observers):
                sig_v[o, at, :] = block[o * ROWS:(o + 1) * ROWS]

    piece_here(0)
    for band in range(bands):
        prepare(band, groups)
    first(0)

    tiles_out = samples // LANES + 1
    lane = lax.broadcasted_iota(jnp.int32, (8, LANES), 1)
    lag = lax.broadcasted_iota(jnp.int32, (8, LANES), 0)
    passed = [lane < lag + j * 8 for j in range(LAGS // 8)]

    def second(depth, o, carry):
        taps = taps_v[o, :, :depth]
        place = place_v[o, :, :depth]
        table = jnp.concatenate(
            [jnp.where(place == jnp.bfloat16(j), taps, jnp.bfloat16(0)) for j in range(LAGS // ROWS)], 0
        )
        lagged = jnp.dot(table, sig_v[o, :depth, :], preferred_element_type=jnp.float32)
        parts = [jnp.zeros((8, LANES), jnp.float32)] * tiles_out
        for j in range(LAGS // 8):
            turned = [
                pltpu.roll(lagged[j * 8:(j + 1) * 8, t * LANES:(t + 1) * LANES], j * 8, 1, stride=1, stride_axis=0)
                for t in range(samples // LANES)
            ]
            before, here = [0.0] + turned, turned + [0.0]
            parts = [part + jnp.where(passed[j], before[t], here[t]) for t, part in enumerate(parts)]
        for t, tile in enumerate(parts):
            part_v[t, at_chunk(o * 8, 8), :] = tile
        return carry

    held = 1
    while held <= groups:
        @pl.when((count > held // 2) & (count <= held))
        def _(held=held):
            for i in range(1, held):
                piece_here(i)
            for band in range(bands, observers // 8):
                prepare(band, held)
            for i in range(1, held):
                first(i)
            if held == groups:
                for o in range(observers):
                    second(held * GB, o, 0)
            else:
                lax.fori_loop(0, observers, functools.partial(second, held * GB), 0, unroll=True)
            for i in range(held, pieces):
                piece_here(i)

        held *= 2

    for t in range(tiles_out):
        total = part_v[t, pl.ds(0, observers, stride=8), :]
        for r in range(1, 8):
            total = total + part_v[t, pl.ds(r, observers, stride=8), :]
        if t < tiles_out - 1:
            main_ref[:, t * LANES:(t + 1) * LANES] = total
        else:
            tail_ref[...] = total


def far_partial(loading, green, delays, offsets, live_groups):
    panels, samples = loading.shape
    observers = green.shape[0]
    blocks = panels // BP
    groups = blocks // GB
    pieces = groups
    operands = (live_groups, loading, green, delays, offsets)
    far = pl.BlockSpec(memory_space=pltpu.HBM)
    vmem = pl.BlockSpec(memory_space=pltpu.VMEM)
    return pl.pallas_call(
        functools.partial(far_kernel, groups),
        out_shape=(
            jax.ShapeDtypeStruct((observers, samples), jnp.float32),
            jax.ShapeDtypeStruct((observers, LAGS), jnp.float32),
        ),
        in_specs=[far] * 5,
        out_specs=(vmem, vmem),
        scratch_shapes=[
            pltpu.SMEM(live_groups.shape, jnp.int32),
            pltpu.VMEM((panels, samples), jnp.bfloat16),
            pltpu.VMEM((observers, panels), jnp.bfloat16),
            pltpu.VMEM((panels // CHUNK, observers, CHUNK), jnp.float32),
            pltpu.VMEM((observers, blocks), jnp.int32),
            pltpu.VMEM((observers, blocks), jnp.int32),
            pltpu.VMEM((observers, ROWS, blocks), jnp.bfloat16),
            pltpu.VMEM((observers, ROWS, blocks), jnp.bfloat16),
            pltpu.VMEM((observers, blocks, samples), jnp.bfloat16),
            pltpu.VMEM((samples // LANES + 1, observers * 8, LANES), jnp.float32),
            pltpu.SemaphoreType.DMA((4,)),
            pltpu.SemaphoreType.DMA((pieces,)),
        ],
        compiler_params=pltpu.CompilerParams(vmem_limit_bytes=24 * 1024 * 1024),
        name="far_partial",
    )(*[pltpu.with_memory_space_constraint(x, pltpu.HBM) for x in operands])


def shards(loading, green, delays, offsets, live_groups):
    main, tail = far_partial(loading, green, delays, offsets, live_groups)
    sectors = lax.axis_size("panel")
    samples = main.shape[1]
    reach = 2 if sectors > 1 else 1
    carried = from_slab_before(tail, 0)
    if reach == 2:
        carried = carried + from_slab_before(tail, 1)
        main = main + from_sector(main, 1)
    carried = jnp.where(lax.axis_index("slab") > 0, carried, 0.0)
    part = main + jnp.pad(carried, ((0, 0), (0, samples - LAGS)))
    while reach < sectors:
        steps = [k * reach for k in (1, 2, 3) if k * reach < sectors]
        part = part + functools.reduce(jnp.add, [from_sector(part, step) for step in steps])
        reach *= len(steps) + 1
    return part


def solution(mesh):
    placed = (
        P(("case", "panel"), "slab"),
        P(("case", "obs"), "panel"),
        P(("case", "obs"), "panel"),
        P(("case", "obs"), "panel"),
        P("case"),
    )
    return jax.shard_map(
        shards, mesh=mesh, in_specs=placed, out_specs=P(("case", "obs"), "slab"), check_vma=False
    )
```

```python
import functools

import jax
import jax.numpy as jnp
from jax import lax
from jax.experimental import pallas as pl
from jax.experimental.pallas import tpu as pltpu
from jax.sharding import PartitionSpec as P

BP = 16
GB = 128
LAGS = 128
TAPS = 8
ROWS = 16
LANES = 128
CHUNK = 256


def from_sector(block, step):
    sectors = lax.axis_size("panel")
    route = [(i, i ^ step) for i in range(sectors)]
    return lax.ppermute(block.astype(jnp.bfloat16), "panel", route).astype(jnp.float32)


def from_slab_before(block, step):
    sectors, slabs = lax.axis_size("panel"), lax.axis_size("slab")
    route = [
        (p * slabs + q, (p ^ step) * slabs + (q + 1) % slabs) for p in range(sectors) for q in range(slabs)
    ]
    return lax.ppermute(block.astype(jnp.bfloat16), ("panel", "slab"), route).astype(jnp.float32)


def weight_lanes():
    lane = lax.broadcasted_iota(jnp.int32, (8, LANES), 1)
    tap = (lane % ROWS).astype(jnp.float32)
    position = 3.0 + (lane // ROWS).astype(jnp.float32) / 8.0
    top = jnp.ones_like(position)
    bottom = jnp.ones_like(position)
    for other in range(TAPS):
        here = tap == other
        top = top * jnp.where(here, 1.0, position - other)
        bottom = bottom * jnp.where(here, 1.0, tap - other)
    return jnp.where(tap < TAPS, top / bottom, 0.0)


def at_chunk(start, size):
    return pl.ds(start if isinstance(start, int) else pl.multiple_of(start, size), size)


def far_kernel(groups, live_hbm, load_hbm, green_hbm, delay_hbm, offset_hbm, main_ref, tail_ref,
               live_s, load_v, green_v, green_f, delay_v, offset_v, taps_v, place_v, sig_v, part_v,
               small_sem, load_sem):
    observers = green_v.shape[0]
    samples = load_v.shape[1]
    panels = load_v.shape[0]
    blocks = panels // BP
    pieces = load_sem.shape[0]
    piece = panels // pieces
    chunk_blocks = CHUNK // BP

    small = [
        pltpu.make_async_copy(src, dst, small_sem.at[i])
        for i, (src, dst) in enumerate(
            [(live_hbm, live_s), (green_hbm, green_v), (delay_hbm, delay_v), (offset_hbm, offset_v)]
        )
    ]
    loads = [
        pltpu.make_async_copy(load_hbm.at[pl.ds(i * piece, piece)], load_v.at[pl.ds(i * piece, piece)], load_sem.at[i])
        for i in range(pieces)
    ]
    for copy in small:
        copy.start()
    loads[0].start()
    weights = weight_lanes()
    for copy in small:
        copy.wait()
    for copy in loads[1:]:
        copy.start()
    count = live_s[lax.axis_index("panel")]

    row = lax.broadcasted_iota(jnp.int32, (ROWS, LANES), 0)

    def prepare(band, held):
        rows = at_chunk(band * 8, 8)
        for g in range(held):
            cols = pl.ds(g * LANES, LANES)
            dead = jnp.where(g < count, 0, -1024)
            delays = delay_v[rows, cols]
            offsets = offset_v[rows, cols]
            for r in range(8):
                o = band * 8 + r
                delay = jnp.broadcast_to(delays[r:r + 1], (ROWS, LANES))
                offset = jnp.broadcast_to(offsets[r:r + 1], (ROWS, LANES))
                entry = ((row - delay) & (ROWS - 1)) + offset * ROWS
                values = [jnp.take_along_axis(weights, entry[h:h + 8], axis=1) for h in (0, 8)]
                taps_v[o, :, cols] = jnp.concatenate(values, 0).astype(jnp.bfloat16)
                place = ((delay - row + (ROWS - 1)) >> 4) + dead
                place_v[o, :, cols] = place.astype(jnp.float32).astype(jnp.bfloat16)

    for c in range(panels // CHUNK):
        green_f[c] = green_v[:, c * CHUNK:(c + 1) * CHUNK].astype(jnp.float32)
    own = lax.broadcasted_iota(jnp.int32, (ROWS, CHUNK), 1) // BP == lax.broadcasted_iota(jnp.int32, (ROWS, CHUNK), 0)
    own = own.astype(jnp.float32).astype(jnp.bfloat16)

    per = piece // CHUNK
    bands = observers // 8 // pieces

    def piece_here(i):
        pltpu.make_async_copy(load_hbm.at[pl.ds(0, piece)], load_v.at[pl.ds(0, piece)], load_sem.at[i]).wait()

    def first(i):
        for c in range(per):
            chunk = i * per + c
            spread = []
            for o in range(observers):
                line = jnp.broadcast_to(green_f[chunk, o:o + 1, :], (ROWS, CHUNK)).astype(jnp.bfloat16)
                spread.append(line * own)
            block = jnp.dot(
                jnp.concatenate(spread, 0),
                load_v[at_chunk(chunk * CHUNK, CHUNK), :],
                preferred_element_type=jnp.float32,
            ).astype(jnp.bfloat16)
            at = at_chunk(chunk * chunk_blocks, chunk_blocks)
            for o in range(observers):
                sig_v[o, at, :] = block[o * ROWS:(o + 1) * ROWS]

    piece_here(0)
    for band in range(bands):
        prepare(band, groups)
    first(0)

    tiles_out = samples // LANES + 1
    lane = lax.broadcasted_iota(jnp.int32, (8, LANES), 1)
    lag = lax.broadcasted_iota(jnp.int32, (8, LANES), 0)
    passed = [lane < lag + j * 8 for j in range(LAGS // 8)]

    def second(depth, o, carry):
        taps = taps_v[o, :, :depth]
        place = place_v[o, :, :depth]
        table = jnp.concatenate(
            [jnp.where(place == jnp.bfloat16(j), taps, jnp.bfloat16(0)) for j in range(LAGS // ROWS)], 0
        )
        lagged = jnp.dot(table, sig_v[o, :depth, :], preferred_element_type=jnp.float32)
        parts = [jnp.zeros((8, LANES), jnp.float32)] * tiles_out
        for j in range(LAGS // 8):
            turned = [
                pltpu.roll(lagged[j * 8:(j + 1) * 8, t * LANES:(t + 1) * LANES], j * 8, 1, stride=1, stride_axis=0)
                for t in range(samples // LANES)
            ]
            before, here = [0.0] + turned, turned + [0.0]
            parts = [part + jnp.where(passed[j], before[t], here[t]) for t, part in enumerate(parts)]
        for t, tile in enumerate(parts):
            part_v[t, at_chunk(o * 8, 8), :] = tile
        return carry

    held = 1
    while held <= groups:
        @pl.when((count > held // 2) & (count <= held))
        def _(held=held):
            for i in range(1, held):
                piece_here(i)
            for band in range(bands, observers // 8):
                prepare(band, held)
            for i in range(1, held):
                first(i)
            if held == groups:
                for o in range(observers):
                    second(held * GB, o, 0)
            else:
                lax.fori_loop(0, observers, functools.partial(second, held * GB), 0, unroll=True)
            for i in range(held, pieces):
                piece_here(i)

        held *= 2

    for t in range(tiles_out):
        total = part_v[t, pl.ds(0, observers, stride=8), :]
        for r in range(1, 8):
            total = total + part_v[t, pl.ds(r, observers, stride=8), :]
        if t < tiles_out - 1:
            main_ref[:, t * LANES:(t + 1) * LANES] = total
        else:
            tail_ref[...] = total


def far_partial(loading, green, delays, offsets, live_groups):
    panels, samples = loading.shape
    observers = green.shape[0]
    blocks = panels // BP
    groups = blocks // GB
    pieces = groups
    operands = (live_groups, loading, green, delays, offsets)
    far = pl.BlockSpec(memory_space=pltpu.HBM)
    vmem = pl.BlockSpec(memory_space=pltpu.VMEM)
    return pl.pallas_call(
        functools.partial(far_kernel, groups),
        out_shape=(
            jax.ShapeDtypeStruct((observers, samples), jnp.float32),
            jax.ShapeDtypeStruct((observers, LAGS), jnp.float32),
        ),
        in_specs=[far] * 5,
        out_specs=(vmem, vmem),
        scratch_shapes=[
            pltpu.SMEM(live_groups.shape, jnp.int32),
            pltpu.VMEM((panels, samples), jnp.bfloat16),
            pltpu.VMEM((observers, panels), jnp.bfloat16),
            pltpu.VMEM((panels // CHUNK, observers, CHUNK), jnp.float32),
            pltpu.VMEM((observers, blocks), jnp.int32),
            pltpu.VMEM((observers, blocks), jnp.int32),
            pltpu.VMEM((observers, ROWS, blocks), jnp.bfloat16),
            pltpu.VMEM((observers, ROWS, blocks), jnp.bfloat16),
            pltpu.VMEM((observers, blocks, samples), jnp.bfloat16),
            pltpu.VMEM((samples // LANES + 1, observers * 8, LANES), jnp.float32),
            pltpu.SemaphoreType.DMA((4,)),
            pltpu.SemaphoreType.DMA((pieces,)),
        ],
        compiler_params=pltpu.CompilerParams(vmem_limit_bytes=24 * 1024 * 1024),
        name="far_partial",
    )(*[pltpu.with_memory_space_constraint(x, pltpu.HBM) for x in operands])


def shards(loading, green, delays, offsets, live_groups):
    main, tail = far_partial(loading, green, delays, offsets, live_groups)
    sectors = lax.axis_size("panel")
    samples = main.shape[1]
    reach = 2 if sectors > 1 else 1
    carried = from_slab_before(tail, 0)
    if reach == 2:
        carried = carried + from_slab_before(tail, 1)
        main = main + from_sector(main, 1)
    carried = jnp.where(lax.axis_index("slab") > 0, carried, 0.0)
    part = main + jnp.pad(carried, ((0, 0), (0, samples - LAGS)))
    while reach < sectors:
        steps = [k * reach for k in (1, 2, 3) if k * reach < sectors]
        part = part + functools.reduce(jnp.add, [from_sector(part, step) for step in steps])
        reach *= len(steps) + 1
    return part


def solution(mesh):
    placed = (
        P(("case", "panel"), "slab"),
        P(("case", "obs"), "panel"),
        P(("case", "obs"), "panel"),
        P(("case", "obs"), "panel"),
        P("case"),
    )
    return jax.shard_map(
        shards, mesh=mesh, in_specs=placed, out_specs=P(("case", "obs"), "slab"), check_vma=False
    )
```
